32 devices in a mesh: group: 2 (over x), dp: 16 (over z, y, core).
Axes of the slice: x: 2, y: 2, z: 4, core: 2. Of those that a mesh axis runs over, the one named last changes fastest.
Arguments:
- acts: bfloat16 [2, 8192, 4096], P(None, ('group', 'dp')), parts along dimension 1, may hold values from -16 to 16
- grads: bfloat16 [2, 8192, 4096], P(None, ('group', 'dp')), parts along dimension 1, may hold values from -16 to 16
- proj_in: bfloat16 [2, 4096, 64], replicated, may hold values from -0.09375 to 0.09375
- proj_out: bfloat16 [2, 4096, 64], replicated, may hold values from -0.09375 to 0.09375
- example_ids: int32 [32, 256], P(('group', 'dp')), parts along dimension 0, may hold values from 0 to 15, never falling along the last dimension, each value on 1 to 32 neighbouring positions
- queries: bfloat16 [2, 256, 4096], P(None, 'dp'), may hold values from -6 to 6
Outputs:
- scores: float32 [512, 256], P(('group', 'dp')), parts along dimension 0
The draws below stay inside these ranges and needn't reach their ends.
There are 2 independent parts, one for each index of `group`. The reference program is written for one: setup_inputs(seed, part) draws one part's arguments, and reference() takes and returns one part's arrays. A program takes and returns all parts, laid end to end along the dimension named above; an argument that names none is the same for every part. Nothing has to cross between parts.
Inputs may be any that keep to these rules, and one draw needn't show every extreme that they name: `example_ids`: each row is non-decreasing, every number 0 to 15 appears, each example has 1 to 32 tokens, one exactly that many.
All inputs are finite; a program needn't handle non-finite values.
Results may differ from the reference program's by a relative error of at most 0.0003.
Values may be sent and summed in bfloat16 or wider, within the bound.
A program may use at most 128 MiB of HBM per device.

```python
import math
import jax
import jax.numpy as jnp
import numpy as np
from jax import lax

D = 4096
R = 64
LAYERS = 2
TOK_DEV = 256
EX_DEV = 16
SHARDS = 16
TOKENS = 4096
EXAMPLES = 256
QUERIES = 256


def rough_rows(key, rise_rate, first_strength, second_strength, third_strength):
    keys = jax.random.split(key, 8)
    noise = jnp.clip(jax.random.normal(keys[0], (LAYERS, TOKENS, D), jnp.float32), -4.0, 4.0)
    spread = jnp.exp(jax.random.uniform(keys[1], (LAYERS, TOKENS, 1), jnp.float32) * jnp.log(3.2))
    position = jnp.arange(TOKENS, dtype=jnp.float32) / TOKENS
    base = jnp.sqrt(1.0 + rise_rate * position)[None, :, None] * spread
    mixed = noise
    total_power = 1.0
    for strength, common_key, loading_key in ((first_strength, keys[2], keys[3]), (second_strength, keys[4], keys[5]), (third_strength, keys[6], keys[7])):
        common = jnp.clip(jax.random.normal(common_key, (LAYERS, 1, D), jnp.float32), -4.0, 4.0)
        loading = jnp.clip(jax.random.normal(loading_key, (LAYERS, TOKENS, 1), jnp.float32), -4.0, 4.0)
        mixed = mixed + strength * loading * common
        total_power = total_power + strength * strength
    values = base * mixed / jnp.sqrt(total_power)
    return jnp.clip(values, -16.0, 16.0).astype(jnp.bfloat16)


def draw_acts(key, part):
    key = jax.random.fold_in(key, 11)
    return rough_rows(key, 2.0, 6.0, 3.0, 2.0)


def draw_grads(key, part):
    key = jax.random.fold_in(key, 23)
    return rough_rows(key, 2.0, 6.0, 3.0, 2.0)


def block_scale(rng, dims, shards, smallest, high):
    def one(dim, blocks):
        steps = jax.random.uniform(jax.random.fold_in(jax.random.fold_in(rng, 6), dim), (blocks,), jnp.float32, smallest / len(shards), high / len(shards))
        return jnp.repeat(jnp.exp(steps), dims[dim] // blocks).reshape((-1,) + (1,) * (len(dims) - dim - 1))

    level = one(*shards[0])
    for cut in shards[1:]:
        level = level * one(*cut)
    return level


def split_up(count, total, most, skew):
    weights = [(1 << 20) // math.isqrt(rank ** skew) + 1 for rank in range(2, count + 1)]
    rest, counts = total - most - (count - 1), [1] * (count - 1)
    while rest > 0:
        movable = [i for i in range(count - 1) if counts[i] < most]
        pool, remaining = sum([weights[i] for i in movable]), rest
        for i in movable:
            addition = min(most - counts[i], max(1, remaining * weights[i] // pool), rest)
            counts[i] = counts[i] + addition
            rest = rest - addition
    return np.array([most] + counts)


def uneven_parts(own_key, number_of, total, bound, skew):
    if number_of == 2:
        one = jax.random.randint(own_key, (), max(1, total - bound), min(bound, total - 1) + 1)
        return jnp.stack([one, total - one])
    sizes = jnp.asarray(split_up(number_of, total, bound, skew), jnp.int32)
    twos = (number_of - 1) // 2
    source_of, sink = sizes[1:1 + 2 * twos:2], sizes[2:2 + 2 * twos:2]
    slack = jnp.minimum(source_of - 1, bound - sink)
    moved = jax.random.randint(jax.random.fold_in(own_key, 1), (twos,), 0, 1 << 20) % (slack + 1)
    sizes = sizes.at[1:1 + 2 * twos:2].set(source_of - moved).at[2:2 + 2 * twos:2].set(sink + moved)
    return sizes[jax.random.permutation(jax.random.fold_in(own_key, 2), number_of)]


def centred(rng, shape, deviation, most, cuts=(), held_as=jnp.bfloat16):
    entries = jax.random.normal(rng, shape, jnp.float32) * deviation
    if len(cuts) > 0:
        entries = block_scale(rng, shape, cuts, -0.22, 0.18) * entries
    return jnp.clip(entries, min=-most, max=most).astype(held_as)


def setup_inputs(seed: int = 0, part: int = 0) -> dict:
    streams_of = jax.random.split(jax.random.key(seed), 7)
    own_keys = jax.random.split(jax.random.fold_in(streams_of[6], part), 7)
    return {
        "acts": draw_acts(jax.random.fold_in(jax.random.fold_in(streams_of[6], part), 71), part),
        "grads": draw_grads(jax.random.fold_in(jax.random.fold_in(streams_of[6], part), 71), part),
        "proj_in": centred(streams_of[2], (LAYERS, D, R), D ** -0.5, 0.09375),
        "proj_out": centred(streams_of[3], (LAYERS, D, R), D ** -0.5, 0.09375),
        "example_ids": jax.vmap(lambda own: jnp.searchsorted(jnp.cumsum(uneven_parts(own, EX_DEV, TOK_DEV, 2 * TOK_DEV // EX_DEV, 1)), jnp.arange(TOK_DEV), side="right"))(jax.random.split(own_keys[4], SHARDS)).reshape((SHARDS, TOK_DEV)).astype(jnp.int32),
        "queries": centred(streams_of[5], (LAYERS, QUERIES, R * R), 1.0, 6.0, ((1, 16),)),
    }


def invert_damped(factor):
    width = factor.shape[0]
    identity = jnp.eye(width, dtype=jnp.float32)
    damped = factor + 0.1 * (jnp.trace(factor) / width) * identity
    lower = jnp.linalg.cholesky(damped)
    return jax.scipy.linalg.cho_solve((lower, True), identity)

def reference(acts, grads, proj_in, proj_out, example_ids, queries):
    highest = lax.Precision.HIGHEST
    onehot = (example_ids[:, None, :] == jnp.arange(EX_DEV, dtype=jnp.int32)[None, :, None]).astype(jnp.float32)
    total = jnp.zeros((EXAMPLES, QUERIES), jnp.float32)
    for layer in range(LAYERS):
        inner = jnp.dot(acts[layer].astype(jnp.float32), proj_in[layer].astype(jnp.float32), preferred_element_type=jnp.float32)
        outer = jnp.dot(grads[layer].astype(jnp.float32), proj_out[layer].astype(jnp.float32), preferred_element_type=jnp.float32)
        act_factor = jnp.dot(inner.T, inner, precision=highest) / TOKENS
        grad_factor = jnp.dot(outer.T, outer, precision=highest) / TOKENS
        inv_act = invert_damped(act_factor)
        inv_grad = invert_damped(grad_factor)
        inner_blocks = inner.reshape(SHARDS, TOK_DEV, R)
        outer_blocks = outer.reshape(SHARDS, TOK_DEV, R)
        weighted = onehot[:, :, :, None] * outer_blocks[:, None, :, :]
        example_grad = jnp.einsum('setr,sti->seri', weighted, inner_blocks, precision=highest).reshape(EXAMPLES, R, R)
        left = jnp.einsum('ij,ejk->eik', inv_grad, example_grad, precision=highest)
        whitened = jnp.einsum('eik,kl->eil', left, inv_act, precision=highest)
        total = total + jnp.dot(whitened.reshape(EXAMPLES, R * R), queries[layer].astype(jnp.float32).T, precision=highest)
    return total * (1.0 / jnp.sqrt(jnp.float32(LAYERS * R * R)))
```

```python
import functools

import jax
import jax.numpy as jnp
from jax import lax
from jax.experimental import pallas as pl
from jax.experimental.pallas import tpu as pltpu
from jax.sharding import PartitionSpec as P

EX_DEV = 16
SLICES = 16
DAMP = 0.1
MESH = pl.DeviceIdType.MESH
HIGHEST = lax.Precision.HIGHEST
NT = (((1,), (1,)), ((), ()))
TN = (((0,), (0,)), ((), ()))


def split(x):
    hi = x.astype(jnp.bfloat16)
    return hi, (x - hi.astype(jnp.float32)).astype(jnp.bfloat16)


def dot(a, b):
    return jnp.dot(a, b, precision=HIGHEST, preferred_element_type=jnp.float32)


def bdot(a, b):
    return jnp.dot(a, b, preferred_element_type=jnp.float32)


def kernel(
    n, folded, acts, grads, pin, pout, ids, queries, out,
    abuf, pbuf, qbuf, gram, rsbuf, xbuf, full,
    load_sem, own_sem, rs_send, rs_recv, x_send, x_recv, ag_send, ag_recv,
    ring_send, ring_recv, chip_send, chip_recv,
):
    layers, tokens, _ = acts.shape
    width = pin.shape[1]
    me = lax.axis_index("dp")
    chips = n // 2
    half = chips // 2
    chip, core = me // 2, me % 2

    def pos_to_dev(p):
        p = (p + chips) % chips
        if folded:
            y = p // half
            z = p * (1 - y) + (chips - 1 - p) * y
            p = 2 * z + y
        return 2 * p + core

    if folded:
        z, y = chip // 2, chip % 2
        pos = z + y * (chips - 1 - 2 * z)
    else:
        pos = chip
    right, left = pos_to_dev(pos + 1), pos_to_dev(pos - 1)
    partner = 2 * chip + (1 - core)

    barrier = pltpu.get_barrier_semaphore()
    for k in range(1, n):
        pl.semaphore_signal(barrier, inc=1, device_id={"dp": (me + k) % n}, device_id_type=MESH)

    loads = []
    for layer in range(layers):
        for side, (data, proj) in enumerate(((acts, pin), (grads, pout))):
            i = 2 * layer + side
            loads.append((
                pltpu.make_async_copy(proj.at[layer], pbuf.at[i], load_sem.at[2 * i]),
                pltpu.make_async_copy(data.at[layer], abuf.at[i], load_sem.at[2 * i + 1]),
            ))
            for copy in loads[-1]:
                copy.start()

    def rows(dev):
        return pl.ds(pl.multiple_of(dev * EX_DEV, EX_DEV), EX_DEV)

    def remote(src, dst, send, recv, dev):
        return pltpu.make_async_remote_copy(
            src_ref=src, dst_ref=dst, send_sem=send, recv_sem=recv,
            device_id={"dp": dev}, device_id_type=MESH,
        )

    def ring(step, way, arriving):
        sign = 1 - 2 * way
        origin = pos_to_dev(pos - sign * (step + (1 if arriving else 0)))
        lay = slice(None) if step < half - 1 else pl.ds(way, 1)
        dst = qbuf.at[lay, rows(origin), :]
        src = queries.at[lay] if step == 0 and not arriving else dst
        return remote(src, dst, ring_send.at[way, step], ring_recv.at[way, step], right if way == 0 else left)

    def on_chip(index, step, way, arriving):
        if index == 0:
            lay, origin = slice(None), me
        else:
            lay = slice(None) if step < half - 1 else pl.ds(way, 1)
            sign = 1 - 2 * way
            origin = pos_to_dev(pos - sign * (step + 1))
        if arriving:
            origin = origin + (1 - 2 * core)
        dst = qbuf.at[lay, rows(origin), :]
        src = queries if index == 0 and not arriving else dst
        return remote(src, dst, chip_send.at[index], chip_recv.at[index], partner)

    def advance(step):
        for way in range(2):
            ring(step, way, True).wait_recv()
            if step + 1 < half:
                ring(step + 1, way, False).start()
            on_chip(1 + 2 * step + way, step, way, False).start()

    pl.semaphore_wait(barrier, n - 1)
    for way in range(2):
        ring(0, way, False).start()
    on_chip(0, 0, 0, False).start()
    own = pltpu.make_async_copy(queries, qbuf.at[:, rows(me), :], own_sem)
    own.start()

    lane = lax.broadcasted_iota(jnp.int32, (1, 2 * width), 1)
    low = lane < width
    tokens_out = []
    for layer in range(layers):
        sides = []
        for side in range(2):
            i = 2 * layer + side
            for copy in loads[i]:
                copy.wait()
            sides.append(lax.dot_general(abuf[i], pbuf[i], NT, preferred_element_type=jnp.float32))
        both = jnp.concatenate(sides, axis=1)
        tokens_out.append(both)
        g = lax.dot_general(both, both, TN, precision=HIGHEST, preferred_element_type=jnp.float32)
        gram[pl.ds(layer * width, width), :] = jnp.where(low, g[:width], g[width:])

    slot = me % SLICES
    block = me - slot

    def slice_of(ref, s):
        return ref.at[pl.ds(pl.multiple_of(8 * s, 8), 8), :]

    peers = [(slot + k) % SLICES for k in range(SLICES)]
    sources = [(slot + SLICES - k) % SLICES for k in range(SLICES)]
    scatter = [
        remote(slice_of(gram, peers[k]), rsbuf.at[k], rs_send.at[k], rs_recv.at[k], block + peers[k])
        for k in range(1, SLICES)
    ]
    for copy in scatter:
        copy.start()
    mine = gram[pl.ds(pl.multiple_of(8 * slot, 8), 8), :]
    advance(0)
    for copy in scatter:
        copy.wait_recv()
    for k in range(1, SLICES):
        mine = mine + rsbuf[k]
    blocks = n // SLICES
    crossing = []
    if blocks > 1:
        xbuf[0] = mine
        for k in range(1, blocks):
            copy = remote(xbuf.at[0], xbuf.at[k], x_send.at[k], x_recv.at[k], (me + k * SLICES) % n)
            copy.start()
            crossing.append(copy)
        for copy in crossing:
            copy.wait_recv()
        home = me // SLICES
        mine = jnp.zeros_like(mine)
        for b in range(blocks):
            mine = mine + xbuf[(home - b + blocks) % blocks]
    full[pl.ds(pl.multiple_of(8 * slot, 8), 8), :] = mine
    gather = [
        remote(slice_of(full, slot), slice_of(full, slot), ag_send.at[k], ag_recv.at[k], block + peers[k])
        for k in range(1, SLICES)
    ]
    for copy in gather:
        copy.start()
    for k in range(1, SLICES):
        there = slice_of(full, sources[k])
        remote(there, there, ag_send.at[k], ag_recv.at[k], block + sources[k]).wait_recv()

    wide = 2 * width
    row = lax.broadcasted_iota(jnp.int32, (wide, wide), 0)
    col = lax.broadcasted_iota(jnp.int32, (wide, wide), 1)
    eye = (row == col).astype(jnp.float32)
    same = (row < width) == (col < width)
    total_tokens = tokens * n
    top, bottom = width + DAMP, DAMP
    mats, scales = [], []
    for layer in range(layers):
        f = full[pl.ds(layer * width, width), :]
        f = jnp.where(same, jnp.concatenate([f, f], axis=0), 0.0) / total_tokens
        diag = jnp.sum(f * eye, axis=0, keepdims=True)
        first = jnp.sum(jnp.where(low, diag, 0.0), axis=1, keepdims=True)
        second = jnp.sum(jnp.where(low, 0.0, diag), axis=1, keepdims=True)
        inv = width / jnp.where(low, first, second)
        scales.append(inv)
        mats.append(f * inv + DAMP * eye)
    t = (top + bottom) / (top - bottom)
    rs = [eye - m * (2.0 / (top + bottom)) for m in mats]
    xs = None
    for doubling in range(7):
        t2 = 2.0 * t * t - 1.0
        up = 2.0 * t * t / t2
        if doubling == 0:
            xs = [(eye + r) * (up * 2.0 / (top + bottom)) for r in rs]
        else:
            xs = [(x + dot(x, r)) * up for x, r in zip(xs, rs)]
        if doubling < 6:
            rs = [dot(r, r) * up - eye * (1.0 / t2) for r in rs]
        t = t2
    advance(1)
    xs = [x + dot(x, eye - dot(m, x)) for m, x in zip(mats, xs)]
    xs = [x * inv for x, inv in zip(xs, scales)]

    onehot = (ids[...] == lax.broadcasted_iota(jnp.int32, (EX_DEV, tokens), 0)).astype(jnp.float32)
    flat = []
    for layer in range(layers):
        w = dot(tokens_out[layer], xs[layer])
        twice = jnp.where(low, w, pltpu.roll(w, width, 1))
        o = w.T[width:]
        rhi, rlo = split(twice)
        lhs = (o[:, None, :] * onehot[None, :, :]).reshape(width * EX_DEV, tokens)
        lhi, llo = split(lhs)
        p = bdot(lhi, rhi) + bdot(lhi, rlo) + bdot(llo, rhi)
        p = p.reshape(width // 2, 2, EX_DEV, wide)
        p = jnp.where(low[None], p[:, 0], p[:, 1])
        p = jnp.concatenate([p[m] for m in range(width // 2)], axis=1)
        hi, lo = split(p)
        flat.append(jnp.concatenate([hi, lo], axis=0))

    for step in range(2, half):
        advance(step)
    own.wait()
    for index in range(2 * half + 1):
        step, way = max(index - 1, 0) // 2, max(index - 1, 0) % 2
        on_chip(index, step, way, True).wait_recv()
    acc = jnp.zeros((2 * EX_DEV, EX_DEV * n), jnp.float32)
    for layer in range(layers):
        acc = acc + lax.dot_general(flat[layer], qbuf[layer], NT, preferred_element_type=jnp.float32)
    out[...] = acc[:EX_DEV] + acc[EX_DEV:]

    for copy in scatter + crossing + gather:
        copy.wait_send()
    for step in range(half):
        for way in range(2):
            ring(step, way, False).wait_send()
    for index in range(2 * half + 1):
        step, way = max(index - 1, 0) // 2, max(index - 1, 0) % 2
        on_chip(index, step, way, False).wait_send()


def shards(n, acts, grads, proj_in, proj_out, example_ids, queries):
    layers, tokens, depth = acts.shape
    width = proj_in.shape[2]
    half = n // 4
    any_spec = pl.BlockSpec(memory_space=pl.ANY)
    vmem = pl.BlockSpec(memory_space=pltpu.VMEM)
    dma = pltpu.SemaphoreType.DMA
    sums = pl.pallas_call(
        functools.partial(kernel, n, n == 16),
        out_shape=jax.ShapeDtypeStruct((EX_DEV, EX_DEV * n), jnp.float32),
        in_specs=[any_spec] * 4 + [vmem, any_spec],
        out_specs=vmem,
        scratch_shapes=[
            pltpu.VMEM((2 * layers, tokens, depth), jnp.bfloat16),
            pltpu.VMEM((2 * layers, width, depth), jnp.bfloat16),
            pltpu.VMEM((layers, EX_DEV * n, width * width), jnp.bfloat16),
            pltpu.VMEM((layers * width, 2 * width), jnp.float32),
            pltpu.VMEM((SLICES, 8, 2 * width), jnp.float32),
            pltpu.VMEM((max(n // SLICES, 1), 8, 2 * width), jnp.float32),
            pltpu.VMEM((layers * width, 2 * width), jnp.float32),
            dma((4 * layers,)),
            dma,
            dma((SLICES,)), dma((SLICES,)),
            dma((n // SLICES,)), dma((n // SLICES,)),
            dma((SLICES,)), dma((SLICES,)),
            dma((2, half)), dma((2, half)),
            dma((2 * half + 1,)), dma((2 * half + 1,)),
        ],
        compiler_params=pltpu.CompilerParams(
            collective_id=0, has_side_effects=True, vmem_limit_bytes=60 * 1024 * 1024
        ),
        name="influence",
    )(
        acts, grads, proj_in.transpose(0, 2, 1), proj_out.transpose(0, 2, 1), example_ids, queries,
    )
    return sums * (1.0 / jnp.sqrt(jnp.float32(layers * width * width)))


def solution(mesh):
    return jax.shard_map(
        functools.partial(shards, mesh.shape["dp"]),
        mesh=mesh,
        in_specs=(
            P(None, ("group", "dp"), None),
            P(None, ("group", "dp"), None),
            P(),
            P(),
            P(("group", "dp"), None),
            P(None, "dp", None),
        ),
        out_specs=P(("group", "dp"), None),
        check_vma=False,
    )
```

```python
import functools

import jax
import jax.numpy as jnp
from jax import lax
from jax.experimental import pallas as pl
from jax.experimental.pallas import tpu as pltpu
from jax.sharding import PartitionSpec as P

EX_DEV = 16
SLICES = 16
DAMP = 0.1
MESH = pl.DeviceIdType.MESH
HIGHEST = lax.Precision.HIGHEST
NT = (((1,), (1,)), ((), ()))
TN = (((0,), (0,)), ((), ()))


def split(x):
    hi = x.astype(jnp.bfloat16)
    return hi, (x - hi.astype(jnp.float32)).astype(jnp.bfloat16)


def dot(a, b):
    return jnp.dot(a, b, precision=HIGHEST, preferred_element_type=jnp.float32)


def bdot(a, b):
    return jnp.dot(a, b, preferred_element_type=jnp.float32)


def kernel(
    n, folded, acts, grads, pin, pout, ids, queries, out,
    abuf, pbuf, qbuf, gram, rsbuf, xbuf, full, xs, rs, outer_t, inner_2, flat,
    load_sem, own_sem, rs_send, rs_recv, x_send, x_recv, ag_send, ag_recv,
    ring_send, ring_recv, chip_send, chip_recv,
):
    layers, tokens, depth = acts.shape
    step_k = 1024
    width = pin.shape[1]
    me = lax.axis_index("dp")
    chips = n // 2
    half = chips // 2
    chip, core = me // 2, me % 2

    def pos_to_dev(p):
        p = (p + chips) % chips
        if folded:
            y = p // half
            z = p * (1 - y) + (chips - 1 - p) * y
            p = 2 * z + y
        return 2 * p + core

    if folded:
        z, y = chip // 2, chip % 2
        pos = z + y * (chips - 1 - 2 * z)
    else:
        pos = chip
    right, left = pos_to_dev(pos + 1), pos_to_dev(pos - 1)
    partner = 2 * chip + (1 - core)

    barrier = pltpu.get_barrier_semaphore()
    for k in range(1, n):
        pl.semaphore_signal(barrier, inc=1, device_id={"dp": (me + k) % n}, device_id_type=MESH)

    loads = []
    for layer in range(layers):
        for side, (data, proj) in enumerate(((acts, pin), (grads, pout))):
            i = 2 * layer + side
            loads.append((
                pltpu.make_async_copy(proj.at[layer], pbuf.at[i], load_sem.at[2 * i]),
                pltpu.make_async_copy(data.at[layer], abuf.at[i], load_sem.at[2 * i + 1]),
            ))
            for copy in loads[-1]:
                copy.start()

    def rows(dev):
        return pl.ds(pl.multiple_of(dev * EX_DEV, EX_DEV), EX_DEV)

    def remote(src, dst, send, recv, dev):
        return pltpu.make_async_remote_copy(
            src_ref=src, dst_ref=dst, send_sem=send, recv_sem=recv,
            device_id={"dp": dev}, device_id_type=MESH,
        )

    def ring(step, way, layer, arriving):
        sign = 1 - 2 * way
        origin = pos_to_dev(pos - sign * (step + (1 if arriving else 0)))
        dst = qbuf.at[layer, rows(origin), :]
        src = queries.at[layer] if step == 0 and not arriving else dst
        sems = ring_send.at[way, step, layer], ring_recv.at[way, step, layer]
        return remote(src, dst, *sems, right if way == 0 else left)

    def carried(step, way):
        if step < half - 1:
            return list(range(layers))
        return list(range(way, layers, 2))

    def on_chip(step, way, layer, arriving):
        sign = 1 - 2 * way
        origin = me if step < 0 else pos_to_dev(pos - sign * (step + 1))
        if arriving:
            origin = origin + (1 - 2 * core)
        dst = qbuf.at[layer, rows(origin), :]
        src = queries.at[layer] if step < 0 and not arriving else dst
        sems = chip_send.at[way, step + 1, layer], chip_recv.at[way, step + 1, layer]
        return remote(src, dst, *sems, partner)

    def advance(step, layer):
        for way in range(2):
            if layer in carried(step, way):
                ring(step, way, layer, True).wait_recv()
                if step + 1 < half and layer in carried(step + 1, way):
                    ring(step + 1, way, layer, False).start()
                on_chip(step, way, layer, False).start()

    lane = lax.broadcasted_iota(jnp.int32, (1, 2 * width), 1)
    low = lane < width
    tokens_out = []

    def project(i):
        def part(c, total):
            at = pl.ds(pl.multiple_of(c * step_k, step_k), step_k)
            return total + lax.dot_general(
                abuf[i, :, at], pbuf[i, :, at], NT, preferred_element_type=jnp.float32
            )

        return lax.fori_loop(0, depth // step_k, part, jnp.zeros((tokens, width), jnp.float32))

    for layer in range(layers):
        sides = []
        for side in range(2):
            i = 2 * layer + side
            for copy in loads[i]:
                copy.wait()
            sides.append(project(i))
        both = jnp.concatenate(sides, axis=1)
        tokens_out.append(both)
        g = lax.dot_general(both, both, TN, precision=HIGHEST, preferred_element_type=jnp.float32)
        gram[pl.ds(layer * width, width), :] = jnp.where(low, g[:width], g[width:])

    pl.semaphore_wait(barrier, n - 1)
    for layer in range(layers):
        for way in range(2):
            ring(0, way, layer, False).start()
    for layer in range(layers):
        on_chip(-1, 0, layer, False).start()
    own = pltpu.make_async_copy(queries, qbuf.at[:, rows(me), :], own_sem)
    own.start()

    slot = me % SLICES
    block = me - slot

    def slice_of(ref, s):
        return ref.at[pl.ds(pl.multiple_of(8 * s, 8), 8), :]

    peers = [(slot + k) % SLICES for k in range(SLICES)]
    sources = [(slot + SLICES - k) % SLICES for k in range(SLICES)]
    scatter = [
        remote(slice_of(gram, peers[k]), rsbuf.at[k], rs_send.at[k], rs_recv.at[k], block + peers[k])
        for k in range(1, SLICES)
    ]
    for copy in scatter:
        copy.start()
    mine = gram[pl.ds(pl.multiple_of(8 * slot, 8), 8), :]
    advance(0, 0)
    advance(0, 1)
    for copy in scatter:
        copy.wait_recv()
    for k in range(1, SLICES):
        mine = mine + rsbuf[k]
    blocks = n // SLICES
    crossing = []
    if blocks > 1:
        xbuf[0] = mine
        for k in range(1, blocks):
            copy = remote(xbuf.at[0], xbuf.at[k], x_send.at[k], x_recv.at[k], (me + k * SLICES) % n)
            copy.start()
            crossing.append(copy)
        for copy in crossing:
            copy.wait_recv()
        home = me // SLICES
        mine = jnp.zeros_like(mine)
        for b in range(blocks):
            mine = mine + xbuf[(home - b + blocks) % blocks]
    full[pl.ds(pl.multiple_of(8 * slot, 8), 8), :] = mine
    gather = [
        remote(slice_of(full, slot), slice_of(full, slot), ag_send.at[k], ag_recv.at[k], block + peers[k])
        for k in range(1, SLICES)
    ]
    for copy in gather:
        copy.start()
    advance(1, 0)
    for k in range(1, SLICES):
        there = slice_of(full, sources[k])
        remote(there, there, ag_send.at[k], ag_recv.at[k], block + sources[k]).wait_recv()

    advance(1, 1)
    wide = 2 * width
    row = lax.broadcasted_iota(jnp.int32, (wide, wide), 0)
    col = lax.broadcasted_iota(jnp.int32, (wide, wide), 1)
    eye = (row == col).astype(jnp.float32)
    same = (row < width) == (col < width)
    total_tokens = tokens * n
    top, bottom = width + DAMP, DAMP
    mats, scales = [], []
    for layer in range(layers):
        f = full[pl.ds(layer * width, width), :]
        f = jnp.where(same, jnp.concatenate([f, f], axis=0), 0.0) / total_tokens
        diag = jnp.sum(f * eye, axis=0, keepdims=True)
        first = jnp.sum(jnp.where(low, diag, 0.0), axis=1, keepdims=True)
        second = jnp.sum(jnp.where(low, 0.0, diag), axis=1, keepdims=True)
        inv = width / jnp.where(low, first, second)
        scales.append(inv)
        mats.append(f * inv + DAMP * eye)
    t = (top + bottom) / (top - bottom)
    up = 2.0 * t * t / (2.0 * t * t - 1.0)
    for layer in range(layers):
        r = eye - mats[layer] * (2.0 / (top + bottom))
        xs[layer] = (eye + r) * (up * 2.0 / (top + bottom))
        rs[layer] = dot(r, r) * up - eye * (up - 1.0)

    def doubling(_, t):
        t2 = 2.0 * t * t - 1.0
        up = 2.0 * t * t / t2
        for layer in range(layers):
            x, r = xs[layer], rs[layer]
            xs[layer] = (x + dot(x, r)) * up
            rs[layer] = dot(r, r) * up - eye * (up - 1.0)
        return t2

    lax.fori_loop(0, 6, doubling, jnp.float32(2.0 * t * t - 1.0))
    advance(2, 0)

    onehot = (ids[...] == lax.broadcasted_iota(jnp.int32, (EX_DEV, tokens), 0)).astype(jnp.float32)
    for layer in range(layers):
        x, m = xs[layer], mats[layer]
        x = (x + dot(x, eye - dot(m, x))) * scales[layer]
        w = dot(tokens_out[layer], x)
        twice = jnp.where(low, w, pltpu.roll(w, width, 1))
        inner_2[layer, 0], inner_2[layer, 1] = split(twice)
        outer_t[layer] = w.T[width:]
    advance(2, 1)

    per = 16

    def example_part(c, _):
        for layer in range(layers):
            o = outer_t[layer, pl.ds(pl.multiple_of(c * per, per), per), :]
            lhs = (o[:, None, :] * onehot[None, :, :]).reshape(per * EX_DEV, tokens)
            lhi, llo = split(lhs)
            rhi, rlo = inner_2[layer, 0], inner_2[layer, 1]
            p = bdot(lhi, rhi) + bdot(lhi, rlo) + bdot(llo, rhi)
            p = p.reshape(per // 2, 2, EX_DEV, wide)
            p = jnp.where(low[None], p[:, 0], p[:, 1])
            p = jnp.concatenate([p[m] for m in range(per // 2)], axis=1)
            hi, lo = split(p)
            at = pl.ds(pl.multiple_of(c * per * width, per * width), per * width)
            flat[layer, :, at] = jnp.concatenate([hi, lo], axis=0)
        return 0

    lax.fori_loop(0, width // per, example_part, 0)

    for step in range(3, half):
        for layer in range(layers):
            advance(step, layer)
    own.wait()
    everything = [(-1, 0, layer) for layer in range(layers)]
    everything += [(step, way, layer) for step in range(half) for way in range(2) for layer in carried(step, way)]
    for item in everything:
        on_chip(*item, True).wait_recv()

    def score_part(c, total):
        at = pl.ds(pl.multiple_of(c * step_k, step_k), step_k)
        for layer in range(layers):
            total = total + lax.dot_general(
                flat[layer, :, at], qbuf[layer, :, at], NT, preferred_element_type=jnp.float32
            )
        return total

    total = lax.fori_loop(
        0, width * width // step_k, score_part, jnp.zeros((2 * EX_DEV, EX_DEV * n), jnp.float32)
    )
    out[...] = total[:EX_DEV] + total[EX_DEV:]

    for copy in scatter + crossing + gather:
        copy.wait_send()
    for item in everything:
        if item[0] >= 0:
            ring(*item, False).wait_send()
        on_chip(*item, False).wait_send()


def shards(n, acts, grads, proj_in, proj_out, example_ids, queries):
    layers, tokens, depth = acts.shape
    width = proj_in.shape[2]
    half = n // 4
    any_spec = pl.BlockSpec(memory_space=pl.ANY)
    vmem = pl.BlockSpec(memory_space=pltpu.VMEM)
    dma = pltpu.SemaphoreType.DMA
    sums = pl.pallas_call(
        functools.partial(kernel, n, n == 16),
        out_shape=jax.ShapeDtypeStruct((EX_DEV, EX_DEV * n), jnp.float32),
        in_specs=[any_spec] * 4 + [vmem, any_spec],
        out_specs=vmem,
        scratch_shapes=[
            pltpu.VMEM((2 * layers, tokens, depth), jnp.bfloat16),
            pltpu.VMEM((2 * layers, width, depth), jnp.bfloat16),
            pltpu.VMEM((layers, EX_DEV * n, width * width), jnp.bfloat16),
            pltpu.VMEM((layers * width, 2 * width), jnp.float32),
            pltpu.VMEM((SLICES, 8, 2 * width), jnp.float32),
            pltpu.VMEM((max(n // SLICES, 1), 8, 2 * width), jnp.float32),
            pltpu.VMEM((layers * width, 2 * width), jnp.float32),
            pltpu.VMEM((layers, 2 * width, 2 * width), jnp.float32),
            pltpu.VMEM((layers, 2 * width, 2 * width), jnp.float32),
            pltpu.VMEM((layers, width, tokens), jnp.float32),
            pltpu.VMEM((layers, 2, tokens, 2 * width), jnp.bfloat16),
            pltpu.VMEM((layers, 2 * EX_DEV, width * width), jnp.bfloat16),
            dma((4 * layers,)),
            dma,
            dma((SLICES,)), dma((SLICES,)),
            dma((n // SLICES,)), dma((n // SLICES,)),
            dma((SLICES,)), dma((SLICES,)),
            dma((2, half, layers)), dma((2, half, layers)),
            dma((2, half + 1, layers)), dma((2, half + 1, layers)),
        ],
        compiler_params=pltpu.CompilerParams(
            collective_id=0, has_side_effects=True, vmem_limit_bytes=60 * 1024 * 1024
        ),
        name="influence",
    )(
        acts, grads, proj_in.transpose(0, 2, 1), proj_out.transpose(0, 2, 1), example_ids, queries,
    )
    return sums * (1.0 / jnp.sqrt(jnp.float32(layers * width * width)))


def solution(mesh):
    return jax.shard_map(
        functools.partial(shards, mesh.shape["dp"]),
        mesh=mesh,
        in_specs=(
            P(None, ("group", "dp"), None),
            P(None, ("group", "dp"), None),
            P(),
            P(),
            P(("group", "dp"), None),
            P(None, "dp", None),
        ),
        out_specs=P(("group", "dp"), None),
        check_vma=False,
    )
```

```python
import functools

import jax
import jax.numpy as jnp
from jax import lax
from jax.experimental import pallas as pl
from jax.experimental.pallas import tpu as pltpu
from jax.sharding import PartitionSpec as P

EX_DEV = 16
SLICES = 16
DAMP = 0.1
MESH = pl.DeviceIdType.MESH
HIGHEST = lax.Precision.HIGHEST
NT = (((1,), (1,)), ((), ()))
TN = (((0,), (0,)), ((), ()))


def split(x):
    hi = x.astype(jnp.bfloat16)
    return hi, (x - hi.astype(jnp.float32)).astype(jnp.bfloat16)


def dot(a, b):
    return jnp.dot(a, b, precision=HIGHEST, preferred_element_type=jnp.float32)


def bdot(a, b):
    return jnp.dot(a, b, preferred_element_type=jnp.float32)


def kernel(
    n, folded, acts, grads, pin, pout, ids, queries, out,
    abuf, pbuf, qbuf, gram, rsbuf, xbuf, full, xs, rs, outer_t, inner_2, flat,
    load_sem, own_sem, rs_send, rs_recv, x_send, x_recv, ag_send, ag_recv,
    ring_send, ring_recv, chip_send, chip_recv, cross_send, cross_recv, last_send, last_recv,
):
    layers, tokens, depth = acts.shape
    step_k = 1024
    width = pin.shape[1]
    me = lax.axis_index("dp")
    chips = n // 2
    half = chips // 2
    chip, core = me // 2, me % 2
    group = lax.axis_index("group")
    side_of = group % 2
    across = group + 1 - 2 * side_of
    cols = width * width
    lacking = 128 * ((cols // 128 + 1) // 3)
    round_cols = cols - lacking

    def columns(start, size):
        return pl.ds(pl.multiple_of(start, 128), size)

    ring_span = columns(side_of * lacking, round_cols)
    give_span = columns(side_of * round_cols, lacking)
    get_span = columns((1 - side_of) * round_cols, lacking)

    def pos_to_dev(p):
        p = (p + chips) % chips
        if folded:
            y = p // half
            z = p * (1 - y) + (chips - 1 - p) * y
            p = 2 * z + y
        return 2 * p + core

    if folded:
        z, y = chip // 2, chip % 2
        pos = z + y * (chips - 1 - 2 * z)
    else:
        pos = chip
    right, left = pos_to_dev(pos + 1), pos_to_dev(pos - 1)
    partner = 2 * chip + (1 - core)

    barrier = pltpu.get_barrier_semaphore()
    for k in range(1, n):
        pl.semaphore_signal(barrier, inc=1, device_id={"dp": (me + k) % n}, device_id_type=MESH)

    pl.semaphore_signal(barrier, inc=1, device_id={"group": across, "dp": me}, device_id_type=MESH)
    loads = []
    for layer in range(layers):
        for side, (data, proj) in enumerate(((acts, pin), (grads, pout))):
            i = 2 * layer + side
            loads.append((
                pltpu.make_async_copy(proj.at[layer], pbuf.at[i], load_sem.at[2 * i]),
                pltpu.make_async_copy(data.at[layer], abuf.at[i], load_sem.at[2 * i + 1]),
            ))
            for copy in loads[-1]:
                copy.start()

    def rows(dev):
        return pl.ds(pl.multiple_of(dev * EX_DEV, EX_DEV), EX_DEV)

    def remote(src, dst, send, recv, dev, to_group=None):
        return pltpu.make_async_remote_copy(
            src_ref=src, dst_ref=dst, send_sem=send, recv_sem=recv,
            device_id={"group": group if to_group is None else to_group, "dp": dev},
            device_id_type=MESH,
        )

    def ring(step, way, layer, arriving):
        sign = 1 - 2 * way
        origin = pos_to_dev(pos - sign * (step + (1 if arriving else 0)))
        dst = qbuf.at[layer, rows(origin), ring_span]
        src = queries.at[layer, :, ring_span] if step == 0 and not arriving else dst
        sems = ring_send.at[way, step, layer], ring_recv.at[way, step, layer]
        return remote(src, dst, *sems, right if way == 0 else left)

    def carried(step, way):
        if step < half - 1:
            return list(range(layers))
        return list(range(way, layers, 2))

    def on_chip(step, way, layer, arriving):
        sign = 1 - 2 * way
        origin = me if step < 0 else pos_to_dev(pos - sign * (step + 1))
        if arriving:
            origin = origin + (1 - 2 * core)
        dst = qbuf.at[layer, rows(origin), slice(None) if step < 0 else ring_span]
        src = queries.at[layer] if step < 0 and not arriving else dst
        sems = chip_send.at[way, step + 1, layer], chip_recv.at[way, step + 1, layer]
        return remote(src, dst, *sems, partner)

    def cross(step, way, layer, arriving):
        origin = pos_to_dev(pos - (1 - 2 * way) * (step + 1))
        dst = qbuf.at[layer, rows(origin), get_span if arriving else give_span]
        return remote(dst, dst, cross_send.at[way, step, layer], cross_recv.at[way, step, layer], me, across)

    def on_chip_crossed(step, way, layer, arriving):
        origin = pos_to_dev(pos - (1 - 2 * way) * (step + 1))
        if arriving:
            origin = origin + (1 - 2 * core)
        dst = qbuf.at[layer, rows(origin), get_span]
        return remote(dst, dst, last_send.at[way, step, layer], last_recv.at[way, step, layer], partner)

    def advance_crossed(step, layer):
        for way in range(2):
            if layer in carried(step, way):
                cross(step, way, layer, True).wait_recv()
                on_chip_crossed(step, way, layer, False).start()

    def advance(step, layer):
        for way in range(2):
            if layer in carried(step, way):
                ring(step, way, layer, True).wait_recv()
                if step + 1 < half and layer in carried(step + 1, way):
                    ring(step + 1, way, layer, False).start()
                cross(step, way, layer, False).start()
                on_chip(step, way, layer, False).start()

    lane = lax.broadcasted_iota(jnp.int32, (1, 2 * width), 1)
    low = lane < width
    tokens_out = []

    def project(i):
        def part(c, total):
            at = pl.ds(pl.multiple_of(c * step_k, step_k), step_k)
            return total + lax.dot_general(
                abuf[i, :, at], pbuf[i, :, at], NT, preferred_element_type=jnp.float32
            )

        return lax.fori_loop(0, depth // step_k, part, jnp.zeros((tokens, width), jnp.float32))

    for layer in range(layers):
        sides = []
        for side in range(2):
            i = 2 * layer + side
            for copy in loads[i]:
                copy.wait()
            sides.append(project(i))
        both = jnp.concatenate(sides, axis=1)
        tokens_out.append(both)
        g = lax.dot_general(both, both, TN, precision=HIGHEST, preferred_element_type=jnp.float32)
        gram[pl.ds(layer * width, width), :] = jnp.where(low, g[:width], g[width:])

    pl.semaphore_wait(barrier, n)
    for layer in range(layers):
        for way in range(2):
            ring(0, way, layer, False).start()
    for layer in range(layers):
        on_chip(-1, 0, layer, False).start()
    own = pltpu.make_async_copy(queries, qbuf.at[:, rows(me), :], own_sem)
    own.start()

    slot = me % SLICES
    block = me - slot

    def slice_of(ref, s):
        return ref.at[pl.ds(pl.multiple_of(8 * s, 8), 8), :]

    peers = [(slot + k) % SLICES for k in range(SLICES)]
    sources = [(slot + SLICES - k) % SLICES for k in range(SLICES)]
    scatter = [
        remote(slice_of(gram, peers[k]), rsbuf.at[k], rs_send.at[k], rs_recv.at[k], block + peers[k])
        for k in range(1, SLICES)
    ]
    for copy in scatter:
        copy.start()
    mine = gram[pl.ds(pl.multiple_of(8 * slot, 8), 8), :]
    advance(0, 0)
    for copy in scatter:
        copy.wait_recv()
    for k in range(1, SLICES):
        mine = mine + rsbuf[k]
    blocks = n // SLICES
    crossing = []
    if blocks > 1:
        xbuf[0] = mine
        for k in range(1, blocks):
            copy = remote(xbuf.at[0], xbuf.at[k], x_send.at[k], x_recv.at[k], (me + k * SLICES) % n)
            copy.start()
            crossing.append(copy)
        for copy in crossing:
            copy.wait_recv()
        home = me // SLICES
        mine = jnp.zeros_like(mine)
        for b in range(blocks):
            mine = mine + xbuf[(home - b + blocks) % blocks]
    full[pl.ds(pl.multiple_of(8 * slot, 8), 8), :] = mine
    gather = [
        remote(slice_of(full, slot), slice_of(full, slot), ag_send.at[k], ag_recv.at[k], block + peers[k])
        for k in range(1, SLICES)
    ]
    for copy in gather:
        copy.start()
    advance(0, 1)
    advance(1, 0)
    for k in range(1, SLICES):
        there = slice_of(full, sources[k])
        remote(there, there, ag_send.at[k], ag_recv.at[k], block + sources[k]).wait_recv()

    wide = 2 * width
    row = lax.broadcasted_iota(jnp.int32, (wide, wide), 0)
    col = lax.broadcasted_iota(jnp.int32, (wide, wide), 1)
    eye = (row == col).astype(jnp.float32)
    same = (row < width) == (col < width)
    total_tokens = tokens * n
    top, bottom = width + DAMP, DAMP
    mats, scales = [], []
    for layer in range(layers):
        f = full[pl.ds(layer * width, width), :]
        f = jnp.where(same, jnp.concatenate([f, f], axis=0), 0.0) / total_tokens
        diag = jnp.sum(f * eye, axis=0, keepdims=True)
        first = jnp.sum(jnp.where(low, diag, 0.0), axis=1, keepdims=True)
        second = jnp.sum(jnp.where(low, 0.0, diag), axis=1, keepdims=True)
        inv = width / jnp.where(low, first, second)
        scales.append(inv)
        mats.append(f * inv + DAMP * eye)
    t = (top + bottom) / (top - bottom)
    up = 2.0 * t * t / (2.0 * t * t - 1.0)
    for layer in range(layers):
        r = eye - mats[layer] * (2.0 / (top + bottom))
        xs[layer] = (eye + r) * (up * 2.0 / (top + bottom))
        rs[layer] = dot(r, r) * up - eye * (up - 1.0)

    def doubling(_, t):
        t2 = 2.0 * t * t - 1.0
        up = 2.0 * t * t / t2
        for layer in range(layers):
            x, r = xs[layer], rs[layer]
            xs[layer] = (x + dot(x, r)) * up
            rs[layer] = dot(r, r) * up - eye * (up - 1.0)
        return t2

    t = lax.fori_loop(0, 3, doubling, jnp.float32(2.0 * t * t - 1.0))
    advance(1, 1)
    lax.fori_loop(0, 3, doubling, t)
    advance(2, 0)
    advance_crossed(0, 0)
    advance_crossed(0, 1)

    onehot = (ids[...] == lax.broadcasted_iota(jnp.int32, (EX_DEV, tokens), 0)).astype(jnp.float32)
    for layer in range(layers):
        x, m = xs[layer], mats[layer]
        x = (x + dot(x, eye - dot(m, x))) * scales[layer]
        w = dot(tokens_out[layer], x)
        twice = jnp.where(low, w, pltpu.roll(w, width, 1))
        inner_2[layer, 0], inner_2[layer, 1] = split(twice)
        outer_t[layer] = w.T[width:]
    advance(2, 1)
    advance_crossed(1, 0)

    per = 16

    def example_part(c, _):
        for layer in range(layers):
            o = outer_t[layer, pl.ds(pl.multiple_of(c * per, per), per), :]
            lhs = (o[:, None, :] * onehot[None, :, :]).reshape(per * EX_DEV, tokens)
            lhi, llo = split(lhs)
            rhi, rlo = inner_2[layer, 0], inner_2[layer, 1]
            p = bdot(lhi, rhi) + bdot(lhi, rlo) + bdot(llo, rhi)
            p = p.reshape(per // 2, 2, EX_DEV, wide)
            p = jnp.where(low[None], p[:, 0], p[:, 1])
            p = jnp.concatenate([p[m] for m in range(per // 2)], axis=1)
            hi, lo = split(p)
            at = pl.ds(pl.multiple_of(c * per * width, per * width), per * width)
            flat[layer, :, at] = jnp.concatenate([hi, lo], axis=0)
        return 0

    lax.fori_loop(0, width // per, example_part, 0)

    for step in range(3, half):
        for layer in range(layers):
            advance(step, layer)
    advance_crossed(1, 1)
    own.wait()
    everything = [(-1, 0, layer) for layer in range(layers)]
    everything += [(step, way, layer) for step in range(half) for way in range(2) for layer in carried(step, way)]
    for item in everything:
        on_chip(*item, True).wait_recv()
    per_score = round_cols // 3

    def score_part(c, total):
        at = columns(side_of * lacking + c * per_score, per_score)
        for layer in range(layers):
            total = total + lax.dot_general(
                flat[layer, :, at], qbuf[layer, :, at], NT, preferred_element_type=jnp.float32
            )
        return total

    for step in range(2, half):
        for layer in range(layers):
            advance_crossed(step, layer)
    total = lax.fori_loop(0, 3, score_part, jnp.zeros((2 * EX_DEV, EX_DEV * n), jnp.float32))
    for item in everything:
        if item[0] >= 0:
            on_chip_crossed(*item, True).wait_recv()
    for layer in range(layers):
        total = total + lax.dot_general(
            flat[layer, :, get_span], qbuf[layer, :, get_span], NT, preferred_element_type=jnp.float32
        )
    out[...] = total[:EX_DEV] + total[EX_DEV:]

    for copy in scatter + crossing + gather:
        copy.wait_send()
    for item in everything:
        if item[0] >= 0:
            ring(*item, False).wait_send()
            cross(*item, False).wait_send()
            on_chip_crossed(*item, False).wait_send()
        on_chip(*item, False).wait_send()


def shards(n, acts, grads, proj_in, proj_out, example_ids, queries):
    layers, tokens, depth = acts.shape
    width = proj_in.shape[2]
    half = n // 4
    any_spec = pl.BlockSpec(memory_space=pl.ANY)
    vmem = pl.BlockSpec(memory_space=pltpu.VMEM)
    dma = pltpu.SemaphoreType.DMA
    sums = pl.pallas_call(
        functools.partial(kernel, n, n == 16),
        out_shape=jax.ShapeDtypeStruct((EX_DEV, EX_DEV * n), jnp.float32),
        in_specs=[any_spec] * 4 + [vmem, any_spec],
        out_specs=vmem,
        scratch_shapes=[
            pltpu.VMEM((2 * layers, tokens, depth), jnp.bfloat16),
            pltpu.VMEM((2 * layers, width, depth), jnp.bfloat16),
            pltpu.VMEM((layers, EX_DEV * n, width * width), jnp.bfloat16),
            pltpu.VMEM((layers * width, 2 * width), jnp.float32),
            pltpu.VMEM((SLICES, 8, 2 * width), jnp.float32),
            pltpu.VMEM((max(n // SLICES, 1), 8, 2 * width), jnp.float32),
            pltpu.VMEM((layers * width, 2 * width), jnp.float32),
            pltpu.VMEM((layers, 2 * width, 2 * width), jnp.float32),
            pltpu.VMEM((layers, 2 * width, 2 * width), jnp.float32),
            pltpu.VMEM((layers, width, tokens), jnp.float32),
            pltpu.VMEM((layers, 2, tokens, 2 * width), jnp.bfloat16),
            pltpu.VMEM((layers, 2 * EX_DEV, width * width), jnp.bfloat16),
            dma((4 * layers,)),
            dma,
            dma((SLICES,)), dma((SLICES,)),
            dma((n // SLICES,)), dma((n // SLICES,)),
            dma((SLICES,)), dma((SLICES,)),
            dma((2, half, layers)), dma((2, half, layers)),
            dma((2, half + 1, layers)), dma((2, half + 1, layers)),
            dma((2, half, layers)), dma((2, half, layers)),
            dma((2, half, layers)), dma((2, half, layers)),
        ],
        compiler_params=pltpu.CompilerParams(
            collective_id=0, has_side_effects=True, vmem_limit_bytes=60 * 1024 * 1024
        ),
        name="influence",
    )(
        acts, grads, proj_in.transpose(0, 2, 1), proj_out.transpose(0, 2, 1), example_ids, queries,
    )
    return sums * (1.0 / jnp.sqrt(jnp.float32(layers * width * width)))


def solution(mesh):
    return jax.shard_map(
        functools.partial(shards, mesh.shape["dp"]),
        mesh=mesh,
        in_specs=(
            P(None, ("group", "dp"), None),
            P(None, ("group", "dp"), None),
            P(),
            P(),
            P(("group", "dp"), None),
            P(None, "dp", None),
        ),
        out_specs=P(("group", "dp"), None),
        check_vma=False,
    )
```

```python
import functools

import jax
import jax.numpy as jnp
from jax import lax
from jax.experimental import pallas as pl
from jax.experimental.pallas import tpu as pltpu
from jax.sharding import PartitionSpec as P

EX_DEV = 16
SLICES = 16
DAMP = 0.1
MESH = pl.DeviceIdType.MESH
HIGHEST = lax.Precision.HIGHEST
NT = (((1,), (1,)), ((), ()))
TN = (((0,), (0,)), ((), ()))


def split(x):
    hi = x.astype(jnp.bfloat16)
    return hi, (x - hi.astype(jnp.float32)).astype(jnp.bfloat16)


def dot(a, b):
    return jnp.dot(a, b, precision=HIGHEST, preferred_element_type=jnp.float32)


def bdot(a, b):
    return jnp.dot(a, b, preferred_element_type=jnp.float32)


def kernel(
    n, folded, acts, grads, pin, pout, ids, queries, out,
    abuf, pbuf, qbuf, gram, rsbuf, xbuf, full, xs, rs, outer_t, inner_2, flat,
    load_sem, own_sem, rs_send, rs_recv, x_send, x_recv, ag_send, ag_recv,
    ring_send, ring_recv, chip_send, chip_recv, cross_send, cross_recv, last_send, last_recv,
):
    layers, tokens, depth = acts.shape
    step_k = 1024
    width = pin.shape[1]
    me = lax.axis_index("dp")
    chips = n // 2
    half = chips // 2
    chip, core = me // 2, me % 2
    group = lax.axis_index("group")
    side_of = group % 2
    across = group + 1 - 2 * side_of
    cols = width * width
    lacking = 128 * ((cols // 128 + 1) // 3)
    round_cols = cols - lacking

    def columns(start, size):
        return pl.ds(pl.multiple_of(start, 128), size)

    middle_span = columns(lacking, cols - 2 * lacking)
    pieces = 2 * layers
    give_span = columns(side_of * round_cols, lacking)
    get_span = columns((1 - side_of) * round_cols, lacking)

    def pos_to_dev(p):
        p = (p + chips) % chips
        if folded:
            y = p // half
            z = p * (1 - y) + (chips - 1 - p) * y
            p = 2 * z + y
        return 2 * p + core

    if folded:
        z, y = chip // 2, chip % 2
        pos = z + y * (chips - 1 - 2 * z)
    else:
        pos = chip
    right, left = pos_to_dev(pos + 1), pos_to_dev(pos - 1)
    partner = 2 * chip + (1 - core)

    barrier = pltpu.get_barrier_semaphore()
    for k in range(1, n):
        pl.semaphore_signal(barrier, inc=1, device_id={"dp": (me + k) % n}, device_id_type=MESH)

    pl.semaphore_signal(barrier, inc=1, device_id={"group": across, "dp": me}, device_id_type=MESH)
    loads = []
    for layer in range(layers):
        for side, (data, proj) in enumerate(((acts, pin), (grads, pout))):
            i = 2 * layer + side
            loads.append((
                pltpu.make_async_copy(proj.at[layer], pbuf.at[i], load_sem.at[2 * i]),
                pltpu.make_async_copy(data.at[layer], abuf.at[i], load_sem.at[2 * i + 1]),
            ))
            for copy in loads[-1]:
                copy.start()

    def rows(dev):
        return pl.ds(pl.multiple_of(dev * EX_DEV, EX_DEV), EX_DEV)

    def remote(src, dst, send, recv, dev, to_group=None):
        return pltpu.make_async_remote_copy(
            src_ref=src, dst_ref=dst, send_sem=send, recv_sem=recv,
            device_id={"group": group if to_group is None else to_group, "dp": dev},
            device_id_type=MESH,
        )

    def span_of(piece):
        return give_span if piece < layers else middle_span

    def ring(step, way, piece, arriving):
        layer = piece % layers
        sign = 1 - 2 * way
        origin = pos_to_dev(pos - sign * (step + (1 if arriving else 0)))
        dst = qbuf.at[layer, rows(origin), span_of(piece)]
        src = queries.at[layer, :, span_of(piece)] if step == 0 and not arriving else dst
        sems = ring_send.at[way, step, piece], ring_recv.at[way, step, piece]
        return remote(src, dst, *sems, right if way == 0 else left)

    def carried(step, way):
        if step < half - 1:
            return list(range(pieces))
        return list(range(way, pieces, 2))

    def on_chip(step, way, piece, arriving):
        sign = 1 - 2 * way
        layer = piece % layers
        origin = me if step < 0 else pos_to_dev(pos - sign * (step + 1))
        if arriving:
            origin = origin + (1 - 2 * core)
        dst = qbuf.at[layer, rows(origin), slice(None) if step < 0 else span_of(piece)]
        src = queries.at[layer] if step < 0 and not arriving else dst
        sems = chip_send.at[way, step + 1, piece], chip_recv.at[way, step + 1, piece]
        return remote(src, dst, *sems, partner)

    def cross(step, way, layer, arriving):
        origin = pos_to_dev(pos - (1 - 2 * way) * (step + 1))
        dst = qbuf.at[layer, rows(origin), get_span if arriving else give_span]
        return remote(dst, dst, cross_send.at[way, step, layer], cross_recv.at[way, step, layer], me, across)

    def on_chip_crossed(step, way, layer, arriving):
        origin = pos_to_dev(pos - (1 - 2 * way) * (step + 1))
        if arriving:
            origin = origin + (1 - 2 * core)
        dst = qbuf.at[layer, rows(origin), get_span]
        return remote(dst, dst, last_send.at[way, step, layer], last_recv.at[way, step, layer], partner)

    def advance_crossed(step, layer):
        for way in range(2):
            if layer in carried(step, way):
                cross(step, way, layer, True).wait_recv()
                on_chip_crossed(step, way, layer, False).start()

    def advance(step, piece):
        for way in range(2):
            if piece in carried(step, way):
                ring(step, way, piece, True).wait_recv()
                if step + 1 < half and piece in carried(step + 1, way):
                    ring(step + 1, way, piece, False).start()
                if piece < layers:
                    cross(step, way, piece, False).start()
                on_chip(step, way, piece, False).start()

    lane = lax.broadcasted_iota(jnp.int32, (1, 2 * width), 1)
    low = lane < width
    tokens_out = []

    def project(i):
        def part(c, total):
            at = pl.ds(pl.multiple_of(c * step_k, step_k), step_k)
            return total + lax.dot_general(
                abuf[i, :, at], pbuf[i, :, at], NT, preferred_element_type=jnp.float32
            )

        return lax.fori_loop(0, depth // step_k, part, jnp.zeros((tokens, width), jnp.float32))

    for layer in range(layers):
        sides = []
        for side in range(2):
            i = 2 * layer + side
            for copy in loads[i]:
                copy.wait()
            sides.append(project(i))
        both = jnp.concatenate(sides, axis=1)
        tokens_out.append(both)
        g = lax.dot_general(both, both, TN, precision=HIGHEST, preferred_element_type=jnp.float32)
        gram[pl.ds(layer * width, width), :] = jnp.where(low, g[:width], g[width:])

    pl.semaphore_wait(barrier, n)
    slot = me % SLICES
    block = me - slot

    def slice_of(ref, s):
        return ref.at[pl.ds(pl.multiple_of(8 * s, 8), 8), :]

    peers = [(slot + k) % SLICES for k in range(SLICES)]
    sources = [(slot + SLICES - k) % SLICES for k in range(SLICES)]
    scatter = [
        remote(slice_of(gram, peers[k]), rsbuf.at[k], rs_send.at[k], rs_recv.at[k], block + peers[k])
        for k in range(1, SLICES)
    ]
    for copy in scatter:
        copy.start()
    for piece in range(pieces):
        for way in range(2):
            ring(0, way, piece, False).start()
    for layer in range(layers):
        on_chip(-1, 0, layer, False).start()
    own = pltpu.make_async_copy(queries, qbuf.at[:, rows(me), :], own_sem)
    own.start()

    mine = gram[pl.ds(pl.multiple_of(8 * slot, 8), 8), :]
    for copy in scatter:
        copy.wait_recv()
    for k in range(1, SLICES):
        mine = mine + rsbuf[k]
    blocks = n // SLICES
    crossing = []
    if blocks > 1:
        xbuf[0] = mine
        for k in range(1, blocks):
            copy = remote(xbuf.at[0], xbuf.at[k], x_send.at[k], x_recv.at[k], (me + k * SLICES) % n)
            copy.start()
            crossing.append(copy)
        for copy in crossing:
            copy.wait_recv()
        home = me // SLICES
        mine = jnp.zeros_like(mine)
        for b in range(blocks):
            mine = mine + xbuf[(home - b + blocks) % blocks]
    full[pl.ds(pl.multiple_of(8 * slot, 8), 8), :] = mine
    gather = [
        remote(slice_of(full, slot), slice_of(full, slot), ag_send.at[k], ag_recv.at[k], block + peers[k])
        for k in range(1, SLICES)
    ]
    for copy in gather:
        copy.start()
    for piece in range(pieces):
        advance(0, piece)
    for k in range(1, SLICES):
        there = slice_of(full, sources[k])
        remote(there, there, ag_send.at[k], ag_recv.at[k], block + sources[k]).wait_recv()

    advance(1, 0)
    advance(1, 1)
    wide = 2 * width
    row = lax.broadcasted_iota(jnp.int32, (wide, wide), 0)
    col = lax.broadcasted_iota(jnp.int32, (wide, wide), 1)
    eye = (row == col).astype(jnp.float32)
    same = (row < width) == (col < width)
    total_tokens = tokens * n
    top, bottom = width + DAMP, DAMP
    mats, scales = [], []
    for layer in range(layers):
        f = full[pl.ds(layer * width, width), :]
        f = jnp.where(same, jnp.concatenate([f, f], axis=0), 0.0) / total_tokens
        diag = jnp.sum(f * eye, axis=0, keepdims=True)
        first = jnp.sum(jnp.where(low, diag, 0.0), axis=1, keepdims=True)
        second = jnp.sum(jnp.where(low, 0.0, diag), axis=1, keepdims=True)
        inv = width / jnp.where(low, first, second)
        scales.append(inv)
        mats.append(f * inv + DAMP * eye)
    t = (top + bottom) / (top - bottom)
    up = 2.0 * t * t / (2.0 * t * t - 1.0)
    for layer in range(layers):
        r = eye - mats[layer] * (2.0 / (top + bottom))
        xs[layer] = (eye + r) * (up * 2.0 / (top + bottom))
        rs[layer] = dot(r, r) * up - eye * (up - 1.0)

    def doubling(_, t):
        t2 = 2.0 * t * t - 1.0
        up = 2.0 * t * t / t2
        for layer in range(layers):
            x, r = xs[layer], rs[layer]
            xs[layer] = (x + dot(x, r)) * up
            rs[layer] = dot(r, r) * up - eye * (up - 1.0)
        return t2

    t = lax.fori_loop(0, 3, doubling, jnp.float32(2.0 * t * t - 1.0))
    for piece in range(2, pieces):
        advance(1, piece)
    advance_crossed(0, 0)
    advance_crossed(0, 1)
    lax.fori_loop(0, 3, doubling, t)
    advance(2, 0)
    advance(2, 1)

    onehot = (ids[...] == lax.broadcasted_iota(jnp.int32, (EX_DEV, tokens), 0)).astype(jnp.float32)
    for layer in range(layers):
        x, m = xs[layer], mats[layer]
        x = (x + dot(x, eye - dot(m, x))) * scales[layer]
        w = dot(tokens_out[layer], x)
        twice = jnp.where(low, w, pltpu.roll(w, width, 1))
        inner_2[layer, 0], inner_2[layer, 1] = split(twice)
        outer_t[layer] = w.T[width:]
    for piece in range(2, pieces):
        advance(2, piece)
    advance_crossed(1, 0)
    advance_crossed(1, 1)

    per = 16

    def example_part(c, _):
        for layer in range(layers):
            o = outer_t[layer, pl.ds(pl.multiple_of(c * per, per), per), :]
            lhs = (o[:, None, :] * onehot[None, :, :]).reshape(per * EX_DEV, tokens)
            lhi, llo = split(lhs)
            rhi, rlo = inner_2[layer, 0], inner_2[layer, 1]
            p = bdot(lhi, rhi) + bdot(lhi, rlo) + bdot(llo, rhi)
            p = p.reshape(per // 2, 2, EX_DEV, wide)
            p = jnp.where(low[None], p[:, 0], p[:, 1])
            p = jnp.concatenate([p[m] for m in range(per // 2)], axis=1)
            hi, lo = split(p)
            at = pl.ds(pl.multiple_of(c * per * width, per * width), per * width)
            flat[layer, :, at] = jnp.concatenate([hi, lo], axis=0)
        return 0

    lax.fori_loop(0, width // per, example_part, 0)

    for step in range(3, half):
        for piece in range(pieces):
            advance(step, piece)
    own.wait()
    everything = [(-1, 0, layer) for layer in range(layers)]
    everything += [(step, way, piece) for step in range(half) for way in range(2) for piece in carried(step, way)]
    for item in everything:
        on_chip(*item, True).wait_recv()
    per_score = round_cols // 3

    def score_part(c, total):
        at = columns(side_of * lacking + c * per_score, per_score)
        for layer in range(layers):
            total = total + lax.dot_general(
                flat[layer, :, at], qbuf[layer, :, at], NT, preferred_element_type=jnp.float32
            )
        return total

    for step in range(2, half):
        for layer in range(layers):
            advance_crossed(step, layer)
    total = lax.fori_loop(0, 3, score_part, jnp.zeros((2 * EX_DEV, EX_DEV * n), jnp.float32))
    for item in everything:
        if item[0] >= 0 and item[2] < layers:
            on_chip_crossed(*item, True).wait_recv()
    for layer in range(layers):
        total = total + lax.dot_general(
            flat[layer, :, get_span], qbuf[layer, :, get_span], NT, preferred_element_type=jnp.float32
        )
    out[...] = total[:EX_DEV] + total[EX_DEV:]

    for copy in scatter + crossing + gather:
        copy.wait_send()
    for item in everything:
        if item[0] >= 0:
            ring(*item, False).wait_send()
        if item[0] >= 0 and item[2] < layers:
            cross(*item, False).wait_send()
            on_chip_crossed(*item, False).wait_send()
        on_chip(*item, False).wait_send()


def shards(n, acts, grads, proj_in, proj_out, example_ids, queries):
    layers, tokens, depth = acts.shape
    width = proj_in.shape[2]
    half = n // 4
    any_spec = pl.BlockSpec(memory_space=pl.ANY)
    vmem = pl.BlockSpec(memory_space=pltpu.VMEM)
    dma = pltpu.SemaphoreType.DMA
    sums = pl.pallas_call(
        functools.partial(kernel, n, n == 16),
        out_shape=jax.ShapeDtypeStruct((EX_DEV, EX_DEV * n), jnp.float32),
        in_specs=[any_spec] * 4 + [vmem, any_spec],
        out_specs=vmem,
        scratch_shapes=[
            pltpu.VMEM((2 * layers, tokens, depth), jnp.bfloat16),
            pltpu.VMEM((2 * layers, width, depth), jnp.bfloat16),
            pltpu.VMEM((layers, EX_DEV * n, width * width), jnp.bfloat16),
            pltpu.VMEM((layers * width, 2 * width), jnp.float32),
            pltpu.VMEM((SLICES, 8, 2 * width), jnp.float32),
            pltpu.VMEM((max(n // SLICES, 1), 8, 2 * width), jnp.float32),
            pltpu.VMEM((layers * width, 2 * width), jnp.float32),
            pltpu.VMEM((layers, 2 * width, 2 * width), jnp.float32),
            pltpu.VMEM((layers, 2 * width, 2 * width), jnp.float32),
            pltpu.VMEM((layers, width, tokens), jnp.float32),
            pltpu.VMEM((layers, 2, tokens, 2 * width), jnp.bfloat16),
            pltpu.VMEM((layers, 2 * EX_DEV, width * width), jnp.bfloat16),
            dma((4 * layers,)),
            dma,
            dma((SLICES,)), dma((SLICES,)),
            dma((n // SLICES,)), dma((n // SLICES,)),
            dma((SLICES,)), dma((SLICES,)),
            dma((2, half, 2 * layers)), dma((2, half, 2 * layers)),
            dma((2, half + 1, 2 * layers)), dma((2, half + 1, 2 * layers)),
            dma((2, half, layers)), dma((2, half, layers)),
            dma((2, half, layers)), dma((2, half, layers)),
        ],
        compiler_params=pltpu.CompilerParams(
            collective_id=0, has_side_effects=True, vmem_limit_bytes=60 * 1024 * 1024
        ),
        name="influence",
    )(
        acts, grads, proj_in.transpose(0, 2, 1), proj_out.transpose(0, 2, 1), example_ids, queries,
    )
    return sums * (1.0 / jnp.sqrt(jnp.float32(layers * width * width)))


def solution(mesh):
    return jax.shard_map(
        functools.partial(shards, mesh.shape["dp"]),
        mesh=mesh,
        in_specs=(
            P(None, ("group", "dp"), None),
            P(None, ("group", "dp"), None),
            P(),
            P(),
            P(("group", "dp"), None),
            P(None, "dp", None),
        ),
        out_specs=P(("group", "dp"), None),
        check_vma=False,
    )
```

```python
import functools

import jax
import jax.numpy as jnp
from jax import lax
from jax.experimental import pallas as pl
from jax.experimental.pallas import tpu as pltpu
from jax.sharding import PartitionSpec as P

EX_DEV = 16
SLICES = 16
DAMP = 0.1
MESH = pl.DeviceIdType.MESH
HIGHEST = lax.Precision.HIGHEST
NT = (((1,), (1,)), ((), ()))
TN = (((0,), (0,)), ((), ()))


def split(x):
    hi = x.astype(jnp.bfloat16)
    return hi, (x - hi.astype(jnp.float32)).astype(jnp.bfloat16)


def dot(a, b):
    return jnp.dot(a, b, precision=HIGHEST, preferred_element_type=jnp.float32)


def bdot(a, b):
    return jnp.dot(a, b, preferred_element_type=jnp.float32)


def kernel(
    n, folded, acts, grads, pin, pout, ids, queries, out,
    abuf, pbuf, qbuf, gram, rsbuf, xbuf, full, xs, rs, outer_t, inner_2, flat,
    load_sem, own_sem, rs_send, rs_recv, x_send, x_recv, ag_send, ag_recv,
    ring_send, ring_recv, chip_send, chip_recv, cross_send, cross_recv, last_send, last_recv,
):
    layers, tokens, depth = acts.shape
    step_k = 1024
    width = pin.shape[1]
    me = lax.axis_index("dp")
    chips = n // 2
    half = chips // 2
    chip, core = me // 2, me % 2
    group = lax.axis_index("group")
    side_of = group % 2
    across = group + 1 - 2 * side_of
    cols = width * width
    lacking = 128 * ((cols // 128 + 1) // 3)
    round_cols = cols - lacking

    def columns(start, size):
        return pl.ds(pl.multiple_of(start, 128), size)

    middle_span = columns(lacking, cols - 2 * lacking)
    pieces = 2 * layers
    give_span = columns(side_of * round_cols, lacking)
    get_span = columns((1 - side_of) * round_cols, lacking)

    def pos_to_dev(p):
        p = (p + chips) % chips
        if folded:
            y = p // half
            z = p * (1 - y) + (chips - 1 - p) * y
            p = 2 * z + y
        return 2 * p + core

    if folded:
        z, y = chip // 2, chip % 2
        pos = z + y * (chips - 1 - 2 * z)
    else:
        pos = chip
    right, left = pos_to_dev(pos + 1), pos_to_dev(pos - 1)
    partner = 2 * chip + (1 - core)

    barrier = pltpu.get_barrier_semaphore()
    for k in range(1, n):
        pl.semaphore_signal(barrier, inc=1, device_id={"dp": (me + k) % n}, device_id_type=MESH)

    pl.semaphore_signal(barrier, inc=1, device_id={"group": across, "dp": me}, device_id_type=MESH)
    loads = []
    for layer in range(layers):
        for side, (data, proj) in enumerate(((acts, pin), (grads, pout))):
            i = 2 * layer + side
            loads.append((
                pltpu.make_async_copy(proj.at[layer], pbuf.at[i], load_sem.at[2 * i]),
                pltpu.make_async_copy(data.at[layer], abuf.at[i], load_sem.at[2 * i + 1]),
            ))
            for copy in loads[-1]:
                copy.start()

    def rows(dev):
        return pl.ds(pl.multiple_of(dev * EX_DEV, EX_DEV), EX_DEV)

    def remote(src, dst, send, recv, dev, to_group=None):
        return pltpu.make_async_remote_copy(
            src_ref=src, dst_ref=dst, send_sem=send, recv_sem=recv,
            device_id={"group": group if to_group is None else to_group, "dp": dev},
            device_id_type=MESH,
        )

    def span_of(piece):
        return give_span if piece < layers else middle_span

    def ring(step, way, piece, arriving):
        layer = piece % layers
        sign = 1 - 2 * way
        origin = pos_to_dev(pos - sign * (step + (1 if arriving else 0)))
        dst = qbuf.at[layer, rows(origin), span_of(piece)]
        src = queries.at[layer, :, span_of(piece)] if step == 0 and not arriving else dst
        sems = ring_send.at[way, step, piece], ring_recv.at[way, step, piece]
        return remote(src, dst, *sems, right if way == 0 else left)

    def carried(step, way):
        if step < half - 1:
            return list(range(pieces))
        return list(range(way, pieces, 2))

    def on_chip(step, way, piece, arriving):
        sign = 1 - 2 * way
        layer = piece % layers
        origin = me if step < 0 else pos_to_dev(pos - sign * (step + 1))
        if arriving:
            origin = origin + (1 - 2 * core)
        dst = qbuf.at[layer, rows(origin), slice(None) if step < 0 else span_of(piece)]
        src = queries.at[layer] if step < 0 and not arriving else dst
        sems = chip_send.at[way, step + 1, piece], chip_recv.at[way, step + 1, piece]
        return remote(src, dst, *sems, partner)

    def cross(step, way, layer, arriving):
        origin = pos_to_dev(pos - (1 - 2 * way) * (step + 1))
        dst = qbuf.at[layer, rows(origin), get_span if arriving else give_span]
        return remote(dst, dst, cross_send.at[way, step, layer], cross_recv.at[way, step, layer], me, across)

    def on_chip_crossed(step, way, layer, arriving):
        origin = pos_to_dev(pos - (1 - 2 * way) * (step + 1))
        if arriving:
            origin = origin + (1 - 2 * core)
        dst = qbuf.at[layer, rows(origin), get_span]
        return remote(dst, dst, last_send.at[way, step, layer], last_recv.at[way, step, layer], partner)

    def advance_crossed(step, layer):
        for way in range(2):
            if layer in carried(step, way):
                cross(step, way, layer, True).wait_recv()
                on_chip_crossed(step, way, layer, False).start()

    def advance(step, piece):
        for way in range(2):
            if piece in carried(step, way):
                ring(step, way, piece, True).wait_recv()
                if step + 1 < half and piece in carried(step + 1, way):
                    ring(step + 1, way, piece, False).start()
                if piece < layers:
                    cross(step, way, piece, False).start()
                on_chip(step, way, piece, False).start()

    lane = lax.broadcasted_iota(jnp.int32, (1, 2 * width), 1)
    low = lane < width
    tokens_out = []

    def project(i):
        def part(c, total):
            at = pl.ds(pl.multiple_of(c * step_k, step_k), step_k)
            return total + lax.dot_general(
                abuf[i, :, at], pbuf[i, :, at], NT, preferred_element_type=jnp.float32
            )

        return lax.fori_loop(0, depth // step_k, part, jnp.zeros((tokens, width), jnp.float32))

    for layer in range(layers):
        sides = []
        for side in range(2):
            i = 2 * layer + side
            for copy in loads[i]:
                copy.wait()
            sides.append(project(i))
        both = jnp.concatenate(sides, axis=1)
        tokens_out.append(both)
        g = lax.dot_general(both, both, TN, precision=HIGHEST, preferred_element_type=jnp.float32)
        gram[pl.ds(layer * width, width), :] = jnp.where(low, g[:width], g[width:])
        if layer == 0:
            pl.semaphore_wait(barrier, n)
            for piece in range(pieces):
                for way in range(2):
                    ring(0, way, piece, False).start()
            for layer in range(layers):
                on_chip(-1, 0, layer, False).start()
            own = pltpu.make_async_copy(queries, qbuf.at[:, rows(me), :], own_sem)
            own.start()

    slot = me % SLICES
    block = me - slot

    def slice_of(ref, s):
        return ref.at[pl.ds(pl.multiple_of(8 * s, 8), 8), :]

    peers = [(slot + k) % SLICES for k in range(SLICES)]
    sources = [(slot + SLICES - k) % SLICES for k in range(SLICES)]
    scatter = [
        remote(slice_of(gram, peers[k]), rsbuf.at[k], rs_send.at[k], rs_recv.at[k], block + peers[k])
        for k in range(1, SLICES)
    ]
    for copy in scatter:
        copy.start()
    mine = gram[pl.ds(pl.multiple_of(8 * slot, 8), 8), :]
    for copy in scatter:
        copy.wait_recv()
    for k in range(1, SLICES):
        mine = mine + rsbuf[k]
    blocks = n // SLICES
    crossing = []
    if blocks > 1:
        xbuf[0] = mine
        for k in range(1, blocks):
            copy = remote(xbuf.at[0], xbuf.at[k], x_send.at[k], x_recv.at[k], (me + k * SLICES) % n)
            copy.start()
            crossing.append(copy)
        for copy in crossing:
            copy.wait_recv()
        home = me // SLICES
        mine = jnp.zeros_like(mine)
        for b in range(blocks):
            mine = mine + xbuf[(home - b + blocks) % blocks]
    full[pl.ds(pl.multiple_of(8 * slot, 8), 8), :] = mine
    gather = [
        remote(slice_of(full, slot), slice_of(full, slot), ag_send.at[k], ag_recv.at[k], block + peers[k])
        for k in range(1, SLICES)
    ]
    for copy in gather:
        copy.start()
    for piece in range(pieces):
        advance(0, piece)
    for k in range(1, SLICES):
        there = slice_of(full, sources[k])
        remote(there, there, ag_send.at[k], ag_recv.at[k], block + sources[k]).wait_recv()

    advance(1, 0)
    advance(1, 1)
    wide = 2 * width
    row = lax.broadcasted_iota(jnp.int32, (wide, wide), 0)
    col = lax.broadcasted_iota(jnp.int32, (wide, wide), 1)
    eye = (row == col).astype(jnp.float32)
    same = (row < width) == (col < width)
    total_tokens = tokens * n
    top, bottom = width + DAMP, DAMP
    mats, scales = [], []
    for layer in range(layers):
        f = full[pl.ds(layer * width, width), :]
        f = jnp.where(same, jnp.concatenate([f, f], axis=0), 0.0) / total_tokens
        diag = jnp.sum(f * eye, axis=0, keepdims=True)
        first = jnp.sum(jnp.where(low, diag, 0.0), axis=1, keepdims=True)
        second = jnp.sum(jnp.where(low, 0.0, diag), axis=1, keepdims=True)
        inv = width / jnp.where(low, first, second)
        scales.append(inv)
        mats.append(f * inv + DAMP * eye)
    t = (top + bottom) / (top - bottom)
    up = 2.0 * t * t / (2.0 * t * t - 1.0)
    for layer in range(layers):
        r = eye - mats[layer] * (2.0 / (top + bottom))
        xs[layer] = (eye + r) * (up * 2.0 / (top + bottom))
        rs[layer] = dot(r, r) * up - eye * (up - 1.0)

    def doubling(_, t):
        t2 = 2.0 * t * t - 1.0
        up = 2.0 * t * t / t2
        for layer in range(layers):
            x, r = xs[layer], rs[layer]
            xs[layer] = (x + dot(x, r)) * up
            rs[layer] = dot(r, r) * up - eye * (up - 1.0)
        return t2

    t = lax.fori_loop(0, 3, doubling, jnp.float32(2.0 * t * t - 1.0))
    for piece in range(2, pieces):
        advance(1, piece)
    advance_crossed(0, 0)
    advance_crossed(0, 1)
    lax.fori_loop(0, 3, doubling, t)
    advance(2, 0)
    advance(2, 1)

    onehot = (ids[...] == lax.broadcasted_iota(jnp.int32, (EX_DEV, tokens), 0)).astype(jnp.float32)
    for layer in range(layers):
        x, m = xs[layer], mats[layer]
        x = (x + dot(x, eye - dot(m, x))) * scales[layer]
        w = dot(tokens_out[layer], x)
        twice = jnp.where(low, w, pltpu.roll(w, width, 1))
        inner_2[layer, 0], inner_2[layer, 1] = split(twice)
        outer_t[layer] = w.T[width:]
    for piece in range(2, pieces):
        advance(2, piece)
    advance_crossed(1, 0)
    advance_crossed(1, 1)

    per = 16

    def example_part(c, _):
        for layer in range(layers):
            o = outer_t[layer, pl.ds(pl.multiple_of(c * per, per), per), :]
            lhs = (o[:, None, :] * onehot[None, :, :]).reshape(per * EX_DEV, tokens)
            lhi, llo = split(lhs)
            rhi, rlo = inner_2[layer, 0], inner_2[layer, 1]
            p = bdot(lhi, rhi) + bdot(lhi, rlo) + bdot(llo, rhi)
            p = p.reshape(per // 2, 2, EX_DEV, wide)
            p = jnp.where(low[None], p[:, 0], p[:, 1])
            p = jnp.concatenate([p[m] for m in range(per // 2)], axis=1)
            hi, lo = split(p)
            at = pl.ds(pl.multiple_of(c * per * width, per * width), per * width)
            flat[layer, :, at] = jnp.concatenate([hi, lo], axis=0)
        return 0

    lax.fori_loop(0, width // per, example_part, 0)

    for step in range(3, half):
        for piece in range(pieces):
            advance(step, piece)
    own.wait()
    everything = [(-1, 0, layer) for layer in range(layers)]
    everything += [(step, way, piece) for step in range(half) for way in range(2) for piece in carried(step, way)]
    for item in everything:
        on_chip(*item, True).wait_recv()
    per_score = round_cols // 3

    def score_part(c, total):
        at = columns(side_of * lacking + c * per_score, per_score)
        for layer in range(layers):
            total = total + lax.dot_general(
                flat[layer, :, at], qbuf[layer, :, at], NT, preferred_element_type=jnp.float32
            )
        return total

    for step in range(2, half):
        for layer in range(layers):
            advance_crossed(step, layer)
    total = lax.fori_loop(0, 3, score_part, jnp.zeros((2 * EX_DEV, EX_DEV * n), jnp.float32))
    for item in everything:
        if item[0] >= 0 and item[2] < layers:
            on_chip_crossed(*item, True).wait_recv()
    for layer in range(layers):
        total = total + lax.dot_general(
            flat[layer, :, get_span], qbuf[layer, :, get_span], NT, preferred_element_type=jnp.float32
        )
    out[...] = total[:EX_DEV] + total[EX_DEV:]

    for copy in scatter + crossing + gather:
        copy.wait_send()
    for item in everything:
        if item[0] >= 0:
            ring(*item, False).wait_send()
        if item[0] >= 0 and item[2] < layers:
            cross(*item, False).wait_send()
            on_chip_crossed(*item, False).wait_send()
        on_chip(*item, False).wait_send()


def shards(n, acts, grads, proj_in, proj_out, example_ids, queries):
    layers, tokens, depth = acts.shape
    width = proj_in.shape[2]
    half = n // 4
    any_spec = pl.BlockSpec(memory_space=pl.ANY)
    vmem = pl.BlockSpec(memory_space=pltpu.VMEM)
    dma = pltpu.SemaphoreType.DMA
    sums = pl.pallas_call(
        functools.partial(kernel, n, n == 16),
        out_shape=jax.ShapeDtypeStruct((EX_DEV, EX_DEV * n), jnp.float32),
        in_specs=[any_spec] * 4 + [vmem, any_spec],
        out_specs=vmem,
        scratch_shapes=[
            pltpu.VMEM((2 * layers, tokens, depth), jnp.bfloat16),
            pltpu.VMEM((2 * layers, width, depth), jnp.bfloat16),
            pltpu.VMEM((layers, EX_DEV * n, width * width), jnp.bfloat16),
            pltpu.VMEM((layers * width, 2 * width), jnp.float32),
            pltpu.VMEM((SLICES, 8, 2 * width), jnp.float32),
            pltpu.VMEM((max(n // SLICES, 1), 8, 2 * width), jnp.float32),
            pltpu.VMEM((layers * width, 2 * width), jnp.float32),
            pltpu.VMEM((layers, 2 * width, 2 * width), jnp.float32),
            pltpu.VMEM((layers, 2 * width, 2 * width), jnp.float32),
            pltpu.VMEM((layers, width, tokens), jnp.float32),
            pltpu.VMEM((layers, 2, tokens, 2 * width), jnp.bfloat16),
            pltpu.VMEM((layers, 2 * EX_DEV, width * width), jnp.bfloat16),
            dma((4 * layers,)),
            dma,
            dma((SLICES,)), dma((SLICES,)),
            dma((n // SLICES,)), dma((n // SLICES,)),
            dma((SLICES,)), dma((SLICES,)),
            dma((2, half, 2 * layers)), dma((2, half, 2 * layers)),
            dma((2, half + 1, 2 * layers)), dma((2, half + 1, 2 * layers)),
            dma((2, half, layers)), dma((2, half, layers)),
            dma((2, half, layers)), dma((2, half, layers)),
        ],
        compiler_params=pltpu.CompilerParams(
            collective_id=0, has_side_effects=True, vmem_limit_bytes=60 * 1024 * 1024
        ),
        name="influence",
    )(
        acts, grads, proj_in.transpose(0, 2, 1), proj_out.transpose(0, 2, 1), example_ids, queries,
    )
    return sums * (1.0 / jnp.sqrt(jnp.float32(layers * width * width)))


def solution(mesh):
    return jax.shard_map(
        functools.partial(shards, mesh.shape["dp"]),
        mesh=mesh,
        in_specs=(
            P(None, ("group", "dp"), None),
            P(None, ("group", "dp"), None),
            P(),
            P(),
            P(("group", "dp"), None),
            P(None, "dp", None),
        ),
        out_specs=P(("group", "dp"), None),
        check_vma=False,
    )
```
